32 devices in a mesh: val: 4 (over y, x), col: 8 (over z, core).
Axes of the slice: x: 2, y: 2, z: 4, core: 2. Of those that a mesh axis runs over, the one named last changes fastest.
Arguments:
- valence_store: float32 [4, 8, 2, 48, 2304], P('val', 'col'), may hold values from -6 to 6
- band_owner: int32 [4], replicated, may hold values from 0 to 7
- valence_energy: float32 [4], P('val'), may hold values from -8 to -1
- cond_bands: float32 [32, 2, 48, 2304], P('col'), may hold values from -6 to 6
- cond_energy: float32 [32], P('col'), may hold values from 0.5 to 10
- gvec_index: int32 [4096], replicated, may hold values from 0 to 110591, as said below
Outputs:
- chi_zero: float32 [2, 256, 4096], P(None, 'val', 'col')
The draws below stay inside these ranges and needn't reach their ends.
Inputs may be any that keep to these rules, and one draw needn't show every extreme that they name: `gvec_index`: distinct grid indices; entry 0 is 0 (the zero vector) and entry 1 is 110591.
All inputs are finite; a program needn't handle non-finite values.
Results may differ from the reference program's by a relative error of at most 0.0038.
Values may be sent and summed in bfloat16 or wider, within the bound.
A program may use at most 256 MiB of HBM per device.

```python
import jax
import jax.numpy as jnp
from jax import lax

L = 48
NG = 4096
C_DEV = 4
ROW_DEV = 64
VB = 4
CB = 32
N_VAL = 4
N_COL = 8


def draw_gvec_index(key, part):
    others = 1 + jax.random.permutation(key, L * L * L - 2)[:NG - 2]
    fixed_ends = jnp.array([0, L * L * L - 1], dtype=jnp.int32)
    return jnp.concatenate([fixed_ends, others.astype(jnp.int32)])


def touch_ends(entries, stream_key, smallest, largest):
    dims = entries.shape
    index_at = [jax.random.randint(jax.random.fold_in(stream_key, axis), (), 0, dims[axis]) for axis in range(len(dims))]
    entries = entries.at[tuple(index_at)].set(smallest)
    longest = dims.index(max(dims))
    index_at[longest] = (index_at[longest] + 1) % dims[longest]
    return entries.at[tuple(index_at)].set(largest)


def level_of(key, extent, shards, low, top_value):
    gain = 1.0
    for position, blocks in shards:
        steps = jax.random.uniform(jax.random.fold_in(jax.random.fold_in(key, 6), position), (blocks,), jnp.float32, low / len(shards), top_value / len(shards))
        gain = gain * jnp.repeat(jnp.exp(steps), extent[position] // blocks).reshape((-1,) + (1,) * (len(extent) - 1 - position))
    return gain


def gaussian(own_key, dims, deviation, most, shards=(), kind=jnp.bfloat16):
    gain = level_of(own_key, dims, shards, -0.22, 0.18) if shards else 1.0
    result = jax.random.normal(own_key, dims, jnp.float32) * deviation * gain
    return jnp.minimum(jnp.maximum(result, -most), most).astype(kind)


def setup_inputs(seed: int = 0) -> dict:
    key_of = jax.random.split(jax.random.key(seed), 7)
    return {
        "valence_store": gaussian(key_of[0], (VB, N_COL, 2, L, L * L), 1.0, 6.0, ((0, 4), (1, 8)), jnp.float32),
        "band_owner": touch_ends(jax.random.randint(key_of[1], (VB,), 0, N_COL), jax.random.fold_in(key_of[1], 1), 0, N_COL - 1).astype(jnp.int32),
        "valence_energy": jnp.clip(-8.0 + 7.0 * jax.random.uniform(key_of[2], (VB,), jnp.float32) ** level_of(key_of[2], (VB,), ((0, 4),), -0.2, 0.2), -8.0, -1.0),
        "cond_bands": gaussian(key_of[3], (CB, 2, L, L * L), 1.0, 6.0, ((0, 8),), jnp.float32),
        "cond_energy": jnp.clip(0.5 + 9.5 * jax.random.uniform(key_of[4], (CB,), jnp.float32) ** level_of(key_of[4], (CB,), ((0, 8),), -0.2, 0.2), 0.5, 10.0),
        "gvec_index": draw_gvec_index(jax.random.fold_in(key_of[6], 71), 0),
    }


def pair_block(valence, cond_block, scaling, gvec_index):
    grid_side = cond_block.shape[2]
    real_part = valence[0] * cond_block[:, 0] + valence[1] * cond_block[:, 1]
    imag_part = valence[0] * cond_block[:, 1] - valence[1] * cond_block[:, 0]
    field = lax.complex(real_part, imag_part).reshape(-1, grid_side, grid_side, grid_side)
    spectrum = jnp.fft.fftn(field, axes=(1, 2, 3)).reshape(field.shape[0], -1)
    picked = jnp.take(spectrum, gvec_index, axis=1)
    scaled_real = scaling[:, None] * jnp.real(picked)
    scaled_imag = scaling[:, None] * jnp.imag(picked)
    return jnp.stack([scaled_real, scaled_imag], 1).astype(jnp.bfloat16)

def reference(valence_store, band_owner, valence_energy, cond_bands, cond_energy, gvec_index):
    val_count = valence_energy.shape[0]
    cond_count = cond_energy.shape[0]
    row_count = ROW_DEV * N_VAL
    constant = (cond_count * val_count) ** (-0.25) * L ** (-1.5)
    blocks = cond_bands.reshape(N_COL, C_DEV, 2, L, L * L)
    energy_blocks = cond_energy.reshape(N_COL, C_DEV)
    real_sum = jnp.zeros((row_count, NG), jnp.float32)
    imag_sum = jnp.zeros((row_count, NG), jnp.float32)
    for band_index in range(val_count):
        valence = valence_store[band_index, band_owner[band_index]]
        valence_level = valence_energy[band_index]

        def add_block(carried, inputs):
            cond_block, energies = inputs
            scaling = jnp.sqrt(2.0 / (energies - valence_level)) * constant
            pairs = pair_block(valence, cond_block, scaling, gvec_index)
            head_real = pairs[:, 0, :row_count]
            head_imag = pairs[:, 1, :row_count]
            real_new = carried[0] + jnp.dot(head_real.T, pairs[:, 0], preferred_element_type=jnp.float32) + jnp.dot(head_imag.T, pairs[:, 1], preferred_element_type=jnp.float32)
            imag_new = carried[1] + jnp.dot(head_imag.T, pairs[:, 0], preferred_element_type=jnp.float32) - jnp.dot(head_real.T, pairs[:, 1], preferred_element_type=jnp.float32)
            return ((real_new, imag_new), None)
        (real_sum, imag_sum), unused = lax.scan(add_block, (real_sum, imag_sum), (blocks, energy_blocks))
    return -jnp.stack([real_sum, imag_sum], 0)
```

```python
import functools
import math

import jax
import jax.numpy as jnp
import ml_dtypes
import numpy as np
from jax import lax
from jax.experimental import pallas as pl
from jax.experimental.pallas import tpu as pltpu
from jax.sharding import PartitionSpec as P

ROW_DEV = 64
LANES = 128
BF16 = jnp.bfloat16
F32 = jnp.float32


def split_table(table):
    high = table.astype(ml_dtypes.bfloat16)
    low = (table - high.astype(np.float64)).astype(ml_dtypes.bfloat16)
    return high, low


def tables(side):
    counter = np.arange(side)
    angles = 2.0 * math.pi * ((counter[:, None] * counter[None, :]) % side) / side
    cosine, sine = np.cos(angles), np.sin(angles)
    first = np.zeros((2, 2, side, 2, LANES))
    for band in range(2):
        span = slice(band * side, (band + 1) * side)
        first[band, 0, :, 0, span] = cosine
        first[band, 1, :, 0, span] = sine
        first[band, 1, :, 1, span] = cosine
        first[band, 0, :, 1, span] = -sine
    first_high, first_low = split_table(first.reshape(4 * side, 2 * LANES))
    both_high, both_low = split_table(np.concatenate([cosine, sine], 0))
    left = np.concatenate([both_high, both_high, both_low], 1)
    return first_high, first_low, left


def picker(side, pairs):
    table = np.zeros((2, pairs, LANES, LANES))
    for part in range(2):
        for pair in range(pairs):
            for band in range(2):
                table[part, pair, band * side : (band + 1) * side, (part * pairs + pair) * 2 + band] = 1.0
    return table.reshape(2 * pairs * LANES, LANES).astype(ml_dtypes.bfloat16)


def split(value):
    high = value.astype(BF16)
    return high, (value - high.astype(F32)).astype(BF16)


def dot(left, right, dims=((1,), (0,))):
    return lax.dot_general(left, right, (dims, ((), ())), preferred_element_type=F32)


def spectrum_kernel(
    side, rows_ref, valence_ref, cond_ref, first_high_ref, first_low_ref, left_ref,
    picker_ref, kx_ref, scale_ref, out_ref, grid_a, grid_b, spots, chosen,
):
    bands = cond_ref.shape[0]
    pairs = bands // 2
    plane = side * side
    half = pairs * LANES
    width = 256

    for pair in range(pairs):
        @pl.loop(0, plane // width)
        def _(step, pair=pair):
            lanes = pl.ds(pl.multiple_of(step * width, width), width)
            v_re, v_im = valence_ref[0, :, lanes], valence_ref[1, :, lanes]
            parts = []
            for band in (2 * pair, 2 * pair + 1):
                c_re, c_im = cond_ref[band, 0, :, lanes], cond_ref[band, 1, :, lanes]
                parts += [v_re * c_re + v_im * c_im, v_re * c_im - v_im * c_re]
            high, low = split(jnp.concatenate(parts, 0).T)
            result = (
                dot(high, first_high_ref[...])
                + dot(low, first_high_ref[...])
                + dot(high, first_low_ref[...])
            )
            rows = pl.ds(pl.multiple_of(step * width, width), width)
            grid_a[rows, pair * LANES : (pair + 1) * LANES] = result[:, :LANES]
            grid_a[rows, half + pair * LANES : half + (pair + 1) * LANES] = result[:, LANES:]

    def turn(block):
        high, low = split(block)
        both = dot(left_ref[...], jnp.concatenate([high, low, high], 0))
        real = both[:side, :half] + both[side:, half:]
        imag = both[:side, half:] - both[side:, :half]
        return real, imag

    @pl.loop(0, side)
    def _(y):
        rows = pl.ds(pl.multiple_of(y * side, side), side)
        real, imag = turn(grid_a[rows, :])
        for pair in range(pairs):
            span = slice(pair * LANES, (pair + 1) * LANES)
            grid_b[pair, rows, :] = real[:, span]
            grid_b[pairs + pair, rows, :] = imag[:, span]

    @pl.loop(0, side)
    def _(kz):
        block = jnp.concatenate(
            [grid_b[part, pl.ds(kz, side, stride=side), :] for part in range(2 * pairs)], 1
        )
        real, imag = turn(block)
        for pair in range(pairs):
            span = slice(pair * LANES, (pair + 1) * LANES)
            base = kz * side * 8
            spots[pl.ds(base + pair, side, stride=8), :] = real[:, span]
            spots[pl.ds(base + pairs + pair, side, stride=8), :] = imag[:, span]

    count = out_ref.shape[1]
    chunk = 512
    lane = lax.broadcasted_iota(jnp.int32, (1, LANES), 1)
    lane = jnp.where(lane < side, lane, jnp.where(lane < 2 * side, lane - side, -1)).astype(F32)

    @pl.loop(0, count // chunk)
    def _(step):
        base = step * chunk

        @pl.loop(0, chunk // 32)
        def _(inner):
            for item in range(32):
                spot = pl.multiple_of(rows_ref[base + inner * 32 + item] * 8, 8)
                to = pl.multiple_of((inner * 32 + item) * 8, 8)
                chosen[pl.ds(to, 8), :] = spots[pl.ds(spot, 8), :]

        where = pl.ds(pl.multiple_of(base, chunk), chunk)
        wanted = jnp.broadcast_to(kx_ref[:, where], (LANES, chunk)).T
        mask = wanted == lane
        total = jnp.zeros((chunk, LANES), F32)
        for part in range(2 * pairs):
            value = jnp.where(mask, chosen[pl.ds(part, chunk, stride=8), :], 0.0)
            high, low = split(value)
            table = picker_ref[part * LANES : (part + 1) * LANES, :]
            total += dot(high, table) + dot(low, table)
        values = total.T[: out_ref.shape[0], :]
        out_ref[:, where] = (values * scale_ref[:, :1]).astype(BF16)


def pair_elements(valence, cond_bands, scaling, gvec_index):
    bands, _, side, plane = cond_bands.shape
    count = gvec_index.shape[0]
    pairs = bands // 2
    first_high, first_low, left = tables(side)
    spot = gvec_index % side * side + gvec_index // side % side
    kx = (gvec_index // plane).astype(F32)[None, :]
    scale = jnp.broadcast_to(jnp.tile(scaling, 2)[:, None], (2 * bands, LANES))
    vmem = pl.BlockSpec(memory_space=pltpu.VMEM)
    return pl.pallas_call(
        functools.partial(spectrum_kernel, side),
        out_shape=jax.ShapeDtypeStruct((2 * bands, count), BF16),
        in_specs=[pl.BlockSpec(memory_space=pltpu.SMEM)] + [vmem] * 8,
        out_specs=vmem,
        scratch_shapes=[
            pltpu.VMEM((plane, 2 * pairs * LANES), F32),
            pltpu.VMEM((2 * pairs, plane, LANES), F32),
            pltpu.VMEM((plane * 8, LANES), F32),
            pltpu.VMEM((512 * 8, LANES), F32),
        ],
        compiler_params=pltpu.CompilerParams(vmem_limit_bytes=48 * 1024 * 1024),
    )(spot, valence, cond_bands, first_high, first_low, left, picker(side, pairs), kx, scale)


def from_root(block, axis, source):
    block = jnp.where(lax.axis_index(axis) == source, block, jnp.zeros_like(block))
    return lax.psum(block, axis)


def local(valence_store, band_owner, valence_energy, cond_bands, cond_energy, gvec_index):
    bands, _, side, plane = cond_bands.shape
    n_val, n_col = lax.axis_size("val"), lax.axis_size("col")
    owner_index = band_owner[lax.axis_index("val")]
    valence = from_root(valence_store[0, 0], "col", owner_index)
    constant = (bands * n_col * n_val) ** (-0.25) * side ** (-1.5)
    scaling = jnp.sqrt(2.0 / (cond_energy - valence_energy[0])) * constant
    picked = pair_elements(valence, cond_bands, scaling, gvec_index)
    count = picked.shape[1]
    cols = count // n_col
    columns = picked.reshape(2 * bands, n_col, cols).transpose(1, 0, 2)
    columns = jnp.broadcast_to(columns[None], (n_val, n_col, 2 * bands, cols))
    rows = picked[:, : ROW_DEV * n_val].reshape(2 * bands, n_val, ROW_DEV).transpose(1, 0, 2)
    rows = jnp.broadcast_to(rows[:, None], (n_val, n_col, 2 * bands, ROW_DEV))
    message = jnp.concatenate([columns, rows], 3).reshape(n_val * n_col, 2 * bands, cols + ROW_DEV)
    message = lax.all_to_all(message, ("val", "col"), split_axis=0, concat_axis=0, tiled=True)
    message = message.reshape(n_val * n_col, 2, bands, cols + ROW_DEV).transpose(1, 0, 2, 3)
    message = message.reshape(2, n_val * n_col * bands, cols + ROW_DEV)
    columns, rows = message[:, :, :cols], message[:, :, cols:]
    row_re, row_im = rows[0], rows[1]
    both = jnp.concatenate([rows[0], rows[1]], 0)
    turned = jnp.concatenate([rows[1], -rows[0]], 0)
    flat = columns.reshape(-1, cols)
    return -jnp.stack([dot(both, flat, ((0,), (0,))), dot(turned, flat, ((0,), (0,)))])


def solution(mesh):
    return jax.shard_map(
        local,
        mesh=mesh,
        in_specs=(
            P("val", "col", None, None, None),
            P(),
            P("val"),
            P("col", None, None, None),
            P("col"),
            P(),
        ),
        out_specs=P(None, "val", "col"),
        check_vma=False,
    )
```

```python
import functools
import math

import jax
import jax.numpy as jnp
import ml_dtypes
import numpy as np
from jax import lax
from jax.experimental import pallas as pl
from jax.experimental.pallas import tpu as pltpu
from jax.sharding import PartitionSpec as P

ROW_DEV = 64
LANES = 128
WIDTH = 256
MESH = pl.DeviceIdType.MESH
BF16 = jnp.bfloat16
F32 = jnp.float32


def split_table(table):
    high = table.astype(ml_dtypes.bfloat16)
    low = (table - high.astype(np.float64)).astype(ml_dtypes.bfloat16)
    return high, low


def tables(side):
    counter = np.arange(side)
    angles = 2.0 * math.pi * ((counter[:, None] * counter[None, :]) % side) / side
    cosine, sine = np.cos(angles), np.sin(angles)
    first = np.zeros((2, 2, side, 2, LANES))
    for band in range(2):
        span = slice(band * side, (band + 1) * side)
        first[band, 0, :, 0, span] = cosine
        first[band, 1, :, 0, span] = sine
        first[band, 1, :, 1, span] = cosine
        first[band, 0, :, 1, span] = -sine
    first_high, first_low = split_table(first.reshape(4 * side, 2 * LANES))
    both_high, both_low = split_table(np.concatenate([cosine, sine], 0))
    left = np.concatenate([both_high, both_high, both_low], 1)
    return first_high, first_low, left


def picker(side, pairs):
    table = np.zeros((2, pairs, LANES, LANES))
    for part in range(2):
        for pair in range(pairs):
            for band in range(2):
                table[part, pair, band * side : (band + 1) * side, (part * pairs + pair) * 2 + band] = 1.0
    return table.reshape(2 * pairs * LANES, LANES).astype(ml_dtypes.bfloat16)


def split(value):
    high = value.astype(BF16)
    return high, (value - high.astype(F32)).astype(BF16)


def dot(left, right, dims=((1,), (0,))):
    return lax.dot_general(left, right, (dims, ((), ())), preferred_element_type=F32)


def spectrum_kernel(
    side, scale_constant, rows_ref, owner_ref, val_energy_ref, energy_ref, store_ref, cond_hbm,
    first_high_ref, first_low_ref, left_ref, picker_ref, kx_ref, out_ref,
    grid_a, grid_b, spots, chosen, cond_ref, streams, mine, valence_ref,
    send_sems, recv_sems, cond_sem,
):
    bands = cond_ref.shape[0]
    pairs = bands // 2
    plane = side * side
    half = pairs * LANES
    chunks = plane // WIDTH

    cond_copy = pltpu.make_async_copy(cond_hbm, cond_ref, cond_sem)
    cond_copy.start()

    n_col = lax.axis_size("col")
    me = lax.axis_index("col")
    chips = n_col // 2
    chip, core = me // 2, me % 2
    sibling = me + 1 - 2 * core
    right = jnp.minimum(me + 2, n_col - 2 + core)
    left = jnp.maximum(me - 2, core)
    has_left, has_right = chip > 0, chip < chips - 1

    barrier = pltpu.get_barrier_semaphore()
    pl.semaphore_signal(barrier, inc=1, device_id={"col": sibling}, device_id_type=MESH)

    @pl.when(has_left)
    def _():
        pl.semaphore_signal(barrier, inc=1, device_id={"col": left}, device_id_type=MESH)

    @pl.when(has_right)
    def _():
        pl.semaphore_signal(barrier, inc=1, device_id={"col": right}, device_id_type=MESH)

    pl.semaphore_wait(barrier, 3 - (chip == 0).astype(jnp.int32) - (chip == chips - 1).astype(jnp.int32))

    def copy(kind, k):
        peer = (sibling, right, left)[kind]
        return pltpu.make_async_remote_copy(
            src_ref=streams.at[kind, 0, k],
            dst_ref=streams.at[kind, 1, k],
            send_sem=send_sems.at[kind, k],
            recv_sem=recv_sems.at[kind, k],
            device_id={"col": peer},
            device_id_type=MESH,
        )

    def final_copy(part, k):
        return pltpu.make_async_remote_copy(
            src_ref=valence_ref.at[part, k],
            dst_ref=valence_ref.at[part, k],
            send_sem=send_sems.at[3, k],
            recv_sem=recv_sems.at[3, k],
            device_id={"col": sibling},
            device_id_type=MESH,
        )

    def lanes_of(k):
        return pl.ds(pl.multiple_of(k * WIDTH, WIDTH), WIDTH)

    gap = jnp.full((1, WIDTH), owner_ref[lax.axis_index("val")] - me).astype(F32)
    owned = jnp.maximum(1.0 - gap * gap, 0.0)

    @pl.loop(0, chunks)
    def _(k):
        streams[0, 0, k] = store_ref[1 - core, :, lanes_of(k)] * owned
        copy(0, k).start()

    @pl.when(jnp.logical_not(has_left))
    def _():
        streams[1, 1] = jnp.zeros((chunks, side, WIDTH), F32)

    @pl.when(jnp.logical_not(has_right))
    def _():
        streams[2, 1] = jnp.zeros((chunks, side, WIDTH), F32)

    def pass_on(kind, k, has_source, has_target):
        @pl.when(has_source)
        def _():
            copy(kind, k).wait_recv()

        @pl.when(has_target)
        def _():
            streams[kind, 0, k] = mine[k] + streams[kind, 1, k]
            copy(kind, k).start()

    def first_axis(k):
        v_re, v_im = valence_ref[0, k], valence_ref[1, k]
        lanes = lanes_of(k)
        for pair in range(pairs):
            parts = []
            for band in (2 * pair, 2 * pair + 1):
                c_re, c_im = cond_ref[band, 0, :, lanes], cond_ref[band, 1, :, lanes]
                parts += [v_re * c_re + v_im * c_im, v_re * c_im - v_im * c_re]
            high, low = split(jnp.concatenate(parts, 0).T)
            result = (
                dot(high, first_high_ref[...])
                + dot(low, first_high_ref[...])
                + dot(high, first_low_ref[...])
            )
            grid_a[lanes, pair * LANES : (pair + 1) * LANES] = result[:, :LANES]
            grid_a[lanes, half + pair * LANES : half + (pair + 1) * LANES] = result[:, LANES:]

    def turn(block):
        high, low = split(block)
        both = dot(left_ref[...], jnp.concatenate([high, low, high], 0))
        real = both[:side, :half] + both[side:, half:]
        imag = both[:side, half:] - both[side:, :half]
        return real, imag

    def last_axis(y):
        rows = pl.ds(pl.multiple_of(y * side, 8), side)
        real, imag = turn(grid_a[rows, :])
        for pair in range(pairs):
            span = slice(pair * LANES, (pair + 1) * LANES)
            grid_b[pair, rows, :] = real[:, span]
            grid_b[pairs + pair, rows, :] = imag[:, span]

    lag = max(1, chips // 2)
    near_left = chip < chips // 2
    right_lag = jnp.where(near_left, 0, lag)
    left_lag = lag - right_lag
    cond_copy.wait()

    @pl.loop(0, chunks + lag + 1)
    def _(step):
        @pl.when(step < chunks)
        def _():
            copy(0, step).wait_recv()
            mine[step] = streams[0, 1, step] + store_ref[core, :, lanes_of(step)] * owned

        @pl.when((step >= right_lag) & (step - right_lag < chunks))
        def _():
            pass_on(1, step - right_lag, has_left, has_right)

        @pl.when((step >= left_lag) & (step - left_lag < chunks))
        def _():
            pass_on(2, step - left_lag, has_right, has_left)

        @pl.when((step >= lag) & (step - lag < chunks))
        def _():
            k = step - lag
            valence_ref[core, k] = mine[k] + streams[1, 1, k] + streams[2, 1, k]
            final_copy(core, k).start()

        @pl.when(step > lag)
        def _():
            k = step - lag - 1
            final_copy(1 - core, k).wait_recv()
            first_axis(k)

            @pl.loop(k * WIDTH // side, (k + 1) * WIDTH // side)
            def _(y):
                last_axis(y)

    @pl.loop(0, side)
    def _(kz):
        block = jnp.concatenate(
            [grid_b[part, pl.ds(kz, side, stride=side), :] for part in range(2 * pairs)], 1
        )
        real, imag = turn(block)
        for pair in range(pairs):
            span = slice(pair * LANES, (pair + 1) * LANES)
            base = kz * side
            spots[pl.ds(base, side), pair, :] = real[:, span]
            spots[pl.ds(base, side), pairs + pair, :] = imag[:, span]

    count = out_ref.shape[1]
    chunk = 512
    row = lax.broadcasted_iota(jnp.int32, (2 * bands, LANES), 0) % bands
    energy = jnp.zeros((2 * bands, LANES), F32)
    for band in range(bands):
        energy = jnp.where(row == band, energy_ref[band], energy)
    scale = jnp.sqrt(2.0 / (energy - val_energy_ref[0])) * scale_constant
    lane = lax.broadcasted_iota(jnp.int32, (1, LANES), 1)
    lane = jnp.where(lane < side, lane, jnp.where(lane < 2 * side, lane - side, -1)).astype(F32)

    @pl.loop(0, count // chunk)
    def _(step):
        base = step * chunk

        @pl.loop(0, chunk // 32)
        def _(inner):
            for item in range(32):
                chosen[inner * 32 + item] = spots[rows_ref[base + inner * 32 + item]]

        where = pl.ds(pl.multiple_of(base, chunk), chunk)
        wanted = jnp.broadcast_to(kx_ref[:, where], (LANES, chunk)).T
        mask = wanted == lane
        total = jnp.zeros((chunk, LANES), F32)
        for part in range(2 * pairs):
            value = jnp.where(mask, chosen[:, part, :], 0.0)
            high, low = split(value)
            table = picker_ref[part * LANES : (part + 1) * LANES, :]
            total += dot(high, table) + dot(low, table)
        values = total.T[: out_ref.shape[0], :]
        out_ref[:, where] = (values * scale[:, :1]).astype(BF16)

    @pl.loop(0, chunks)
    def _(k):
        copy(0, k).wait_send()
        final_copy(core, k).wait_send()

        @pl.when(has_right)
        def _():
            copy(1, k).wait_send()

        @pl.when(has_left)
        def _():
            copy(2, k).wait_send()


def pair_elements(store, owner, val_energy, cond_bands, cond_energy, gvec_index):
    bands, _, side, plane = cond_bands.shape
    count = gvec_index.shape[0]
    pairs = bands // 2
    chunks = plane // WIDTH
    first_high, first_low, left = tables(side)
    spot = gvec_index % side * side + gvec_index // side % side
    kx = (gvec_index // plane).astype(F32)[None, :]
    total_bands = bands * lax.axis_size("col") * lax.axis_size("val")
    constant = total_bands ** (-0.25) * side ** (-1.5)
    vmem = pl.BlockSpec(memory_space=pltpu.VMEM)
    smem = pl.BlockSpec(memory_space=pltpu.SMEM)
    return pl.pallas_call(
        functools.partial(spectrum_kernel, side, constant),
        out_shape=jax.ShapeDtypeStruct((2 * bands, count), BF16),
        in_specs=[smem] * 4 + [vmem, pl.BlockSpec(memory_space=pl.ANY)] + [vmem] * 5,
        out_specs=vmem,
        scratch_shapes=[
            pltpu.VMEM((plane, 2 * pairs * LANES), F32),
            pltpu.VMEM((2 * pairs, plane, LANES), F32),
            pltpu.VMEM((plane, 2 * pairs, LANES), F32),
            pltpu.VMEM((512, 2 * pairs, LANES), F32),
            pltpu.VMEM(cond_bands.shape, F32),
            pltpu.VMEM((3, 2, chunks, side, WIDTH), F32),
            pltpu.VMEM((chunks, side, WIDTH), F32),
            pltpu.VMEM((2, chunks, side, WIDTH), F32),
            pltpu.SemaphoreType.DMA((4, chunks)),
            pltpu.SemaphoreType.DMA((4, chunks)),
            pltpu.SemaphoreType.DMA,
        ],
        compiler_params=pltpu.CompilerParams(
            vmem_limit_bytes=60 * 1024 * 1024, collective_id=0, has_side_effects=True
        ),
    )(
        spot, owner, val_energy, cond_energy, store, cond_bands,
        first_high, first_low, left, picker(side, pairs), kx,
    )


def local(valence_store, band_owner, valence_energy, cond_bands, cond_energy, gvec_index):
    bands, _, side, plane = cond_bands.shape
    n_val, n_col = lax.axis_size("val"), lax.axis_size("col")
    picked = pair_elements(
        valence_store[0, 0], band_owner, valence_energy, cond_bands, cond_energy, gvec_index
    )
    count = picked.shape[1]
    cols = count // n_col
    columns = picked.reshape(2 * bands, n_col, cols).transpose(1, 0, 2)
    columns = jnp.broadcast_to(columns[None], (n_val, n_col, 2 * bands, cols))
    rows = picked[:, : ROW_DEV * n_val].reshape(2 * bands, n_val, ROW_DEV).transpose(1, 0, 2)
    rows = jnp.broadcast_to(rows[:, None], (n_val, n_col, 2 * bands, ROW_DEV))
    message = jnp.concatenate([columns, rows], 3).reshape(n_val * n_col, 2 * bands, cols + ROW_DEV)
    message = lax.all_to_all(message, ("val", "col"), split_axis=0, concat_axis=0, tiled=True)
    message = message.reshape(n_val * n_col, 2, bands, cols + ROW_DEV).transpose(1, 0, 2, 3)
    message = message.reshape(2, n_val * n_col * bands, cols + ROW_DEV)
    columns, rows = message[:, :, :cols], message[:, :, cols:]
    row_re, row_im = rows[0], rows[1]
    both = jnp.concatenate([rows[0], rows[1]], 0)
    turned = jnp.concatenate([rows[1], -rows[0]], 0)
    flat = columns.reshape(-1, cols)
    return -jnp.stack([dot(both, flat, ((0,), (0,))), dot(turned, flat, ((0,), (0,)))])


def solution(mesh):
    return jax.shard_map(
        local,
        mesh=mesh,
        in_specs=(
            P("val", "col", None, None, None),
            P(),
            P("val"),
            P("col", None, None, None),
            P("col"),
            P(),
        ),
        out_specs=P(None, "val", "col"),
        check_vma=False,
    )
```

```python
import functools
import math

import jax
import jax.numpy as jnp
import ml_dtypes
import numpy as np
from jax import lax
from jax.experimental import pallas as pl
from jax.experimental.pallas import tpu as pltpu
from jax.sharding import PartitionSpec as P

ROW_DEV = 64
LANES = 128
WIDTH = 256
MESH = pl.DeviceIdType.MESH
BF16 = jnp.bfloat16
F32 = jnp.float32


def split_table(table):
    high = table.astype(ml_dtypes.bfloat16)
    low = (table - high.astype(np.float64)).astype(ml_dtypes.bfloat16)
    return high, low


def tables(side):
    counter = np.arange(side)
    angles = 2.0 * math.pi * ((counter[:, None] * counter[None, :]) % side) / side
    cosine, sine = np.cos(angles), np.sin(angles)
    first = np.zeros((2, 2, side, 2, LANES))
    for band in range(2):
        span = slice(band * side, (band + 1) * side)
        first[band, 0, :, 0, span] = cosine
        first[band, 1, :, 0, span] = sine
        first[band, 1, :, 1, span] = cosine
        first[band, 0, :, 1, span] = -sine
    first_high, first_low = split_table(first.reshape(4 * side, 2 * LANES))
    both_high, both_low = split_table(np.concatenate([cosine, sine], 0))
    left = np.concatenate([both_high, both_high, both_low], 1)
    return first_high, first_low, left


def picker(side, pairs):
    table = np.zeros((2, pairs, LANES, LANES))
    for part in range(2):
        for pair in range(pairs):
            for band in range(2):
                table[part, pair, band * side : (band + 1) * side, (part * pairs + pair) * 2 + band] = 1.0
    return table.reshape(2 * pairs * LANES, LANES).astype(ml_dtypes.bfloat16)


def split(value):
    high = value.astype(BF16)
    return high, (value - high.astype(F32)).astype(BF16)


def dot(left, right, dims=((1,), (0,))):
    return lax.dot_general(left, right, (dims, ((), ())), preferred_element_type=F32)


def turn(side, left_ref, block):
    half = block.shape[1] // 2
    high, low = split(block)
    both = dot(left_ref[...], jnp.concatenate([high, low, high], 0))
    real = both[:side, :half] + both[side:, half:]
    imag = both[:side, half:] - both[side:, :half]
    return real, imag


def spread_kernel(
    side, owner_ref, store_ref, cond_hbm, first_high_ref, first_low_ref, left_ref, grid_b,
    grid_a, cond_ref, streams, mine, valence_ref, send_sems, recv_sems, cond_sem,
):
    bands = cond_ref.shape[0]
    pairs = bands // 2
    plane = side * side
    half = pairs * LANES
    chunks = plane // WIDTH

    cond_copy = pltpu.make_async_copy(cond_hbm, cond_ref, cond_sem)
    cond_copy.start()

    n_col = lax.axis_size("col")
    me = lax.axis_index("col")
    chips = n_col // 2
    chip, core = me // 2, me % 2
    sibling = me + 1 - 2 * core
    right = jnp.minimum(me + 2, n_col - 2 + core)
    left = jnp.maximum(me - 2, core)
    has_left, has_right = chip > 0, chip < chips - 1

    barrier = pltpu.get_barrier_semaphore()
    pl.semaphore_signal(barrier, inc=1, device_id={"col": sibling}, device_id_type=MESH)

    @pl.when(has_left)
    def _():
        pl.semaphore_signal(barrier, inc=1, device_id={"col": left}, device_id_type=MESH)

    @pl.when(has_right)
    def _():
        pl.semaphore_signal(barrier, inc=1, device_id={"col": right}, device_id_type=MESH)

    pl.semaphore_wait(barrier, 3 - (chip == 0).astype(jnp.int32) - (chip == chips - 1).astype(jnp.int32))

    def copy(kind, k):
        peer = (sibling, right, left)[kind]
        return pltpu.make_async_remote_copy(
            src_ref=streams.at[kind, 0, k],
            dst_ref=streams.at[kind, 1, k],
            send_sem=send_sems.at[kind, k],
            recv_sem=recv_sems.at[kind, k],
            device_id={"col": peer},
            device_id_type=MESH,
        )

    def final_copy(part, k):
        return pltpu.make_async_remote_copy(
            src_ref=valence_ref.at[part, k],
            dst_ref=valence_ref.at[part, k],
            send_sem=send_sems.at[3, k],
            recv_sem=recv_sems.at[3, k],
            device_id={"col": sibling},
            device_id_type=MESH,
        )

    def lanes_of(k):
        return pl.ds(pl.multiple_of(k * WIDTH, WIDTH), WIDTH)

    gap = jnp.full((1, WIDTH), owner_ref[lax.axis_index("val")] - me).astype(F32)
    owned = jnp.maximum(1.0 - gap * gap, 0.0)

    @pl.loop(0, chunks)
    def _(k):
        streams[0, 0, k] = store_ref[1 - core, :, lanes_of(k)] * owned
        copy(0, k).start()

    @pl.when(jnp.logical_not(has_left))
    def _():
        streams[1, 1] = jnp.zeros((chunks, side, WIDTH), F32)

    @pl.when(jnp.logical_not(has_right))
    def _():
        streams[2, 1] = jnp.zeros((chunks, side, WIDTH), F32)

    def pass_on(kind, k, has_source, has_target):
        @pl.when(has_source)
        def _():
            copy(kind, k).wait_recv()

        @pl.when(has_target)
        def _():
            streams[kind, 0, k] = mine[k] + streams[kind, 1, k]
            copy(kind, k).start()

    def first_axis(k):
        v_re, v_im = valence_ref[0, k], valence_ref[1, k]
        lanes = lanes_of(k)
        for pair in range(pairs):
            parts = []
            for band in (2 * pair, 2 * pair + 1):
                c_re, c_im = cond_ref[band, 0, :, lanes], cond_ref[band, 1, :, lanes]
                parts += [v_re * c_re + v_im * c_im, v_re * c_im - v_im * c_re]
            high, low = split(jnp.concatenate(parts, 0).T)
            result = (
                dot(high, first_high_ref[...])
                + dot(low, first_high_ref[...])
                + dot(high, first_low_ref[...])
            )
            grid_a[lanes, pair * LANES : (pair + 1) * LANES] = result[:, :LANES]
            grid_a[lanes, half + pair * LANES : half + (pair + 1) * LANES] = result[:, LANES:]

    def last_axis(y):
        rows = pl.ds(pl.multiple_of(y * side, 8), side)
        real, imag = turn(side, left_ref, grid_a[rows, :])
        for pair in range(pairs):
            span = slice(pair * LANES, (pair + 1) * LANES)
            grid_b[pair, rows, :] = real[:, span]
            grid_b[pairs + pair, rows, :] = imag[:, span]

    lag = max(1, chips // 2)
    near_left = chip < chips // 2
    right_lag = jnp.where(near_left, 0, lag)
    left_lag = lag - right_lag
    cond_copy.wait()

    @pl.loop(0, chunks + lag + 1)
    def _(step):
        @pl.when(step < chunks)
        def _():
            copy(0, step).wait_recv()
            mine[step] = streams[0, 1, step] + store_ref[core, :, lanes_of(step)] * owned

        @pl.when((step >= right_lag) & (step - right_lag < chunks))
        def _():
            pass_on(1, step - right_lag, has_left, has_right)

        @pl.when((step >= left_lag) & (step - left_lag < chunks))
        def _():
            pass_on(2, step - left_lag, has_right, has_left)

        @pl.when((step >= lag) & (step - lag < chunks))
        def _():
            k = step - lag
            valence_ref[core, k] = mine[k] + streams[1, 1, k] + streams[2, 1, k]
            final_copy(core, k).start()

        @pl.when(step > lag)
        def _():
            k = step - lag - 1
            final_copy(1 - core, k).wait_recv()
            first_axis(k)

            @pl.loop(k * WIDTH // side, (k + 1) * WIDTH // side)
            def _(y):
                last_axis(y)

    @pl.loop(0, chunks)
    def _(k):
        copy(0, k).wait_send()
        final_copy(core, k).wait_send()

        @pl.when(has_right)
        def _():
            copy(1, k).wait_send()

        @pl.when(has_left)
        def _():
            copy(2, k).wait_send()


def pick_kernel(
    side, bands, scale_constant, rows_ref, val_energy_ref, energy_ref, grid_b, left_ref,
    picker_ref, kx_ref, out_ref, spots, chosen,
):
    pairs = bands // 2

    @pl.loop(0, side)
    def _(kz):
        block = jnp.concatenate(
            [grid_b[part, pl.ds(kz, side, stride=side), :] for part in range(2 * pairs)], 1
        )
        real, imag = turn(side, left_ref, block)
        for pair in range(pairs):
            span = slice(pair * LANES, (pair + 1) * LANES)
            base = kz * side * 8
            spots[pl.ds(base + pair, side, stride=8), :] = real[:, span]
            spots[pl.ds(base + pairs + pair, side, stride=8), :] = imag[:, span]

    count = out_ref.shape[1]
    chunk = 512
    row = lax.broadcasted_iota(jnp.int32, (2 * bands, LANES), 0) % bands
    energy = jnp.zeros((2 * bands, LANES), F32)
    for band in range(bands):
        energy = jnp.where(row == band, energy_ref[band], energy)
    scale = jnp.sqrt(2.0 / (energy - val_energy_ref[0])) * scale_constant
    lane = lax.broadcasted_iota(jnp.int32, (1, LANES), 1)
    lane = jnp.where(lane < side, lane, jnp.where(lane < 2 * side, lane - side, -1)).astype(F32)

    @pl.loop(0, count // chunk)
    def _(step):
        base = step * chunk

        @pl.loop(0, chunk // 32)
        def _(inner):
            for item in range(32):
                spot = pl.multiple_of(rows_ref[base + inner * 32 + item] * 8, 8)
                to = pl.multiple_of((inner * 32 + item) * 8, 8)
                chosen[pl.ds(to, 8), :] = spots[pl.ds(spot, 8), :]

        where = pl.ds(pl.multiple_of(base, chunk), chunk)
        wanted = jnp.broadcast_to(kx_ref[:, where], (LANES, chunk)).T
        mask = wanted == lane
        total = jnp.zeros((chunk, LANES), F32)
        for part in range(2 * pairs):
            value = jnp.where(mask, chosen[pl.ds(part, chunk, stride=8), :], 0.0)
            high, low = split(value)
            table = picker_ref[part * LANES : (part + 1) * LANES, :]
            total += dot(high, table) + dot(low, table)
        values = total.T[: out_ref.shape[0], :]
        out_ref[:, where] = (values * scale[:, :1]).astype(BF16)


def pair_elements(store, owner, val_energy, cond_bands, cond_energy, gvec_index):
    bands, _, side, plane = cond_bands.shape
    count = gvec_index.shape[0]
    pairs = bands // 2
    chunks = plane // WIDTH
    first_high, first_low, left = tables(side)
    spot = gvec_index % side * side + gvec_index // side % side
    kx = (gvec_index // plane).astype(F32)[None, :]
    total_bands = bands * lax.axis_size("col") * lax.axis_size("val")
    constant = total_bands ** (-0.25) * side ** (-1.5)
    vmem = pl.BlockSpec(memory_space=pltpu.VMEM)
    smem = pl.BlockSpec(memory_space=pltpu.SMEM)
    grid = pl.pallas_call(
        functools.partial(spread_kernel, side),
        out_shape=jax.ShapeDtypeStruct((2 * pairs, plane, LANES), F32),
        in_specs=[smem, vmem, pl.BlockSpec(memory_space=pl.ANY)] + [vmem] * 3,
        out_specs=vmem,
        scratch_shapes=[
            pltpu.VMEM((plane, 2 * pairs * LANES), F32),
            pltpu.VMEM(cond_bands.shape, F32),
            pltpu.VMEM((3, 2, chunks, side, WIDTH), F32),
            pltpu.VMEM((chunks, side, WIDTH), F32),
            pltpu.VMEM((2, chunks, side, WIDTH), F32),
            pltpu.SemaphoreType.DMA((4, chunks)),
            pltpu.SemaphoreType.DMA((4, chunks)),
            pltpu.SemaphoreType.DMA,
        ],
        compiler_params=pltpu.CompilerParams(
            vmem_limit_bytes=32 * 1024 * 1024, collective_id=0, has_side_effects=True
        ),
    )(owner, store, cond_bands, first_high, first_low, left)
    return pl.pallas_call(
        functools.partial(pick_kernel, side, bands, constant),
        out_shape=jax.ShapeDtypeStruct((2 * bands, count), BF16),
        in_specs=[smem] * 3 + [vmem] * 4,
        out_specs=vmem,
        scratch_shapes=[
            pltpu.VMEM((plane * 8, LANES), F32),
            pltpu.VMEM((512 * 8, LANES), F32),
        ],
        compiler_params=pltpu.CompilerParams(vmem_limit_bytes=32 * 1024 * 1024),
    )(spot, val_energy, cond_energy, grid, left, picker(side, pairs), kx)


def local(valence_store, band_owner, valence_energy, cond_bands, cond_energy, gvec_index):
    bands, _, side, plane = cond_bands.shape
    n_val, n_col = lax.axis_size("val"), lax.axis_size("col")
    picked = pair_elements(
        valence_store[0, 0], band_owner, valence_energy, cond_bands, cond_energy, gvec_index
    )
    count = picked.shape[1]
    cols = count // n_col
    columns = picked.reshape(2 * bands, n_col, cols).transpose(1, 0, 2)
    columns = jnp.broadcast_to(columns[None], (n_val, n_col, 2 * bands, cols))
    rows = picked[:, : ROW_DEV * n_val].reshape(2 * bands, n_val, ROW_DEV).transpose(1, 0, 2)
    rows = jnp.broadcast_to(rows[:, None], (n_val, n_col, 2 * bands, ROW_DEV))
    message = jnp.concatenate([columns, rows], 3).reshape(n_val * n_col, 2 * bands, cols + ROW_DEV)
    message = lax.all_to_all(message, ("val", "col"), split_axis=0, concat_axis=0, tiled=True)
    message = message.reshape(n_val * n_col, 2, bands, cols + ROW_DEV).transpose(1, 0, 2, 3)
    message = message.reshape(2, n_val * n_col * bands, cols + ROW_DEV)
    columns, rows = message[:, :, :cols], message[:, :, cols:]
    row_re, row_im = rows[0], rows[1]
    both = jnp.concatenate([rows[0], rows[1]], 0)
    turned = jnp.concatenate([rows[1], -rows[0]], 0)
    flat = columns.reshape(-1, cols)
    return -jnp.stack([dot(both, flat, ((0,), (0,))), dot(turned, flat, ((0,), (0,)))])


def solution(mesh):
    return jax.shard_map(
        local,
        mesh=mesh,
        in_specs=(
            P("val", "col", None, None, None),
            P(),
            P("val"),
            P("col", None, None, None),
            P("col"),
            P(),
        ),
        out_specs=P(None, "val", "col"),
        check_vma=False,
    )
```

```python
import functools
import math

import jax
import jax.numpy as jnp
import ml_dtypes
import numpy as np
from jax import lax
from jax.experimental import pallas as pl
from jax.experimental.pallas import tpu as pltpu
from jax.sharding import PartitionSpec as P

ROW_DEV = 64
LANES = 128
WIDTH = 256
MESH = pl.DeviceIdType.MESH
BF16 = jnp.bfloat16
F32 = jnp.float32


def split_table(table):
    high = table.astype(ml_dtypes.bfloat16)
    low = (table - high.astype(np.float64)).astype(ml_dtypes.bfloat16)
    return high, low


def tables(side):
    counter = np.arange(side)
    angles = 2.0 * math.pi * ((counter[:, None] * counter[None, :]) % side) / side
    cosine, sine = np.cos(angles), np.sin(angles)
    first = np.zeros((2, 2, side, 2, LANES))
    for band in range(2):
        span = slice(band * side, (band + 1) * side)
        first[band, 0, :, 0, span] = cosine
        first[band, 1, :, 0, span] = sine
        first[band, 1, :, 1, span] = cosine
        first[band, 0, :, 1, span] = -sine
    first_high, first_low = split_table(first.reshape(4 * side, 2 * LANES))
    both_high, both_low = split_table(np.concatenate([cosine, sine], 0))
    left = np.concatenate([both_high, both_high, both_low], 1)
    return first_high, first_low, left


def picker(side, pairs):
    table = np.zeros((2, pairs, LANES, LANES))
    for part in range(2):
        for pair in range(pairs):
            for band in range(2):
                table[part, pair, band * side : (band + 1) * side, (part * pairs + pair) * 2 + band] = 1.0
    return table.reshape(2 * pairs * LANES, LANES).astype(ml_dtypes.bfloat16)


def split(value):
    high = value.astype(BF16)
    return high, (value - high.astype(F32)).astype(BF16)


def dot(left, right, dims=((1,), (0,))):
    return lax.dot_general(left, right, (dims, ((), ())), preferred_element_type=F32)


def turn(side, left_ref, block):
    half = block.shape[1] // 2
    high, low = split(block)
    both = dot(left_ref[...], jnp.concatenate([high, low, high], 0))
    real = both[:side, :half] + both[side:, half:]
    imag = both[:side, half:] - both[side:, :half]
    return real, imag


def spread_kernel(
    side, owner_ref, store_ref, cond_hbm, first_high_ref, first_low_ref, left_ref, grid_b,
    grid_a, cond_ref, streams, mine, valence_ref, send_sems, recv_sems, cond_sem,
):
    bands = cond_ref.shape[0]
    pairs = bands // 2
    plane = side * side
    half = pairs * LANES
    chunks = plane // WIDTH

    cond_copy = pltpu.make_async_copy(cond_hbm, cond_ref, cond_sem)
    cond_copy.start()

    n_col = lax.axis_size("col")
    me = lax.axis_index("col")
    chips = n_col // 2
    chip, core = me // 2, me % 2
    sibling = me + 1 - 2 * core
    right = jnp.minimum(me + 2, n_col - 2 + core)
    left = jnp.maximum(me - 2, core)
    has_left, has_right = chip > 0, chip < chips - 1

    barrier = pltpu.get_barrier_semaphore()
    pl.semaphore_signal(barrier, inc=1, device_id={"col": sibling}, device_id_type=MESH)

    @pl.when(has_left)
    def _():
        pl.semaphore_signal(barrier, inc=1, device_id={"col": left}, device_id_type=MESH)

    @pl.when(has_right)
    def _():
        pl.semaphore_signal(barrier, inc=1, device_id={"col": right}, device_id_type=MESH)

    pl.semaphore_wait(barrier, 3 - (chip == 0).astype(jnp.int32) - (chip == chips - 1).astype(jnp.int32))

    def copy(kind, k):
        peer = (sibling, right, left)[kind]
        return pltpu.make_async_remote_copy(
            src_ref=streams.at[kind, 0, k],
            dst_ref=streams.at[kind, 1, k],
            send_sem=send_sems.at[kind, k],
            recv_sem=recv_sems.at[kind, k],
            device_id={"col": peer},
            device_id_type=MESH,
        )

    def final_copy(part, k):
        return pltpu.make_async_remote_copy(
            src_ref=valence_ref.at[part, k],
            dst_ref=valence_ref.at[part, k],
            send_sem=send_sems.at[3, k],
            recv_sem=recv_sems.at[3, k],
            device_id={"col": sibling},
            device_id_type=MESH,
        )

    def lanes_of(k):
        return pl.ds(pl.multiple_of(k * WIDTH, WIDTH), WIDTH)

    gap = jnp.full((1, WIDTH), owner_ref[lax.axis_index("val")] - me).astype(F32)
    owned = jnp.maximum(1.0 - gap * gap, 0.0)

    @pl.loop(0, chunks)
    def _(k):
        streams[0, 0, k] = store_ref[1 - core, :, lanes_of(k)] * owned
        copy(0, k).start()

    @pl.when(jnp.logical_not(has_left))
    def _():
        streams[1, 1] = jnp.zeros((chunks, side, WIDTH), F32)

    @pl.when(jnp.logical_not(has_right))
    def _():
        streams[2, 1] = jnp.zeros((chunks, side, WIDTH), F32)

    def pass_on(kind, k, has_source, has_target):
        @pl.when(has_source)
        def _():
            copy(kind, k).wait_recv()

        @pl.when(has_target)
        def _():
            streams[kind, 0, k] = mine[k] + streams[kind, 1, k]
            copy(kind, k).start()

    def first_axis(k):
        v_re, v_im = valence_ref[0, k], valence_ref[1, k]
        lanes = lanes_of(k)
        for pair in range(pairs):
            parts = []
            for band in (2 * pair, 2 * pair + 1):
                c_re, c_im = cond_ref[band, 0, :, lanes], cond_ref[band, 1, :, lanes]
                parts += [v_re * c_re + v_im * c_im, v_re * c_im - v_im * c_re]
            high, low = split(jnp.concatenate(parts, 0).T)
            result = (
                dot(high, first_high_ref[...])
                + dot(low, first_high_ref[...])
                + dot(high, first_low_ref[...])
            )
            grid_a[lanes, pair * LANES : (pair + 1) * LANES] = result[:, :LANES]
            grid_a[lanes, half + pair * LANES : half + (pair + 1) * LANES] = result[:, LANES:]

    def last_axis(y):
        rows = pl.ds(pl.multiple_of(y * side, 8), side)
        real, imag = turn(side, left_ref, grid_a[rows, :])
        for pair in range(pairs):
            span = slice(pair * LANES, (pair + 1) * LANES)
            grid_b[pair, rows, :] = real[:, span]
            grid_b[pairs + pair, rows, :] = imag[:, span]

    right_lag = 2 * chip
    left_lag = 2 * (chips - 1 - chip)
    lag = jnp.maximum(right_lag, left_lag)
    cond_copy.wait()

    @pl.loop(0, chunks + lag + 1)
    def _(step):
        @pl.when(step < chunks)
        def _():
            copy(0, step).wait_recv()
            mine[step] = streams[0, 1, step] + store_ref[core, :, lanes_of(step)] * owned

        @pl.when((step >= right_lag) & (step - right_lag < chunks))
        def _():
            pass_on(1, step - right_lag, has_left, has_right)

        @pl.when((step >= left_lag) & (step - left_lag < chunks))
        def _():
            pass_on(2, step - left_lag, has_right, has_left)

        @pl.when((step >= lag) & (step - lag < chunks))
        def _():
            k = step - lag
            valence_ref[core, k] = mine[k] + streams[1, 1, k] + streams[2, 1, k]
            final_copy(core, k).start()

        @pl.when(step > lag)
        def _():
            k = step - lag - 1
            final_copy(1 - core, k).wait_recv()
            first_axis(k)

            @pl.loop(k * WIDTH // side, (k + 1) * WIDTH // side)
            def _(y):
                last_axis(y)

    @pl.loop(0, chunks)
    def _(k):
        copy(0, k).wait_send()
        final_copy(core, k).wait_send()

        @pl.when(has_right)
        def _():
            copy(1, k).wait_send()

        @pl.when(has_left)
        def _():
            copy(2, k).wait_send()


def pick_kernel(
    side, bands, scale_constant, rows_ref, val_energy_ref, energy_ref, grid_b, left_ref,
    picker_ref, kx_ref, out_ref, spots, chosen,
):
    pairs = bands // 2

    @pl.loop(0, side)
    def _(kz):
        block = jnp.concatenate(
            [grid_b[part, pl.ds(kz, side, stride=side), :] for part in range(2 * pairs)], 1
        )
        real, imag = turn(side, left_ref, block)
        for pair in range(pairs):
            span = slice(pair * LANES, (pair + 1) * LANES)
            base = kz * side * 8
            spots[pl.ds(base + pair, side, stride=8), :] = real[:, span]
            spots[pl.ds(base + pairs + pair, side, stride=8), :] = imag[:, span]

    count = out_ref.shape[1]
    chunk = 512
    row = lax.broadcasted_iota(jnp.int32, (2 * bands, LANES), 0) % bands
    energy = jnp.zeros((2 * bands, LANES), F32)
    for band in range(bands):
        energy = jnp.where(row == band, energy_ref[band], energy)
    scale = jnp.sqrt(2.0 / (energy - val_energy_ref[0])) * scale_constant
    lane = lax.broadcasted_iota(jnp.int32, (1, LANES), 1)
    lane = jnp.where(lane < side, lane, jnp.where(lane < 2 * side, lane - side, -1)).astype(F32)

    @pl.loop(0, count // chunk)
    def _(step):
        base = step * chunk

        @pl.loop(0, chunk // 32)
        def _(inner):
            for item in range(32):
                spot = pl.multiple_of(rows_ref[base + inner * 32 + item] * 8, 8)
                to = pl.multiple_of((inner * 32 + item) * 8, 8)
                chosen[pl.ds(to, 8), :] = spots[pl.ds(spot, 8), :]

        where = pl.ds(pl.multiple_of(base, chunk), chunk)
        wanted = jnp.broadcast_to(kx_ref[:, where], (LANES, chunk)).T
        mask = wanted == lane
        total = jnp.zeros((chunk, LANES), F32)
        for part in range(2 * pairs):
            value = jnp.where(mask, chosen[pl.ds(part, chunk, stride=8), :], 0.0)
            high, low = split(value)
            table = picker_ref[part * LANES : (part + 1) * LANES, :]
            total += dot(high, table) + dot(low, table)
        values = total.T[: out_ref.shape[0], :]
        out_ref[:, where] = (values * scale[:, :1]).astype(BF16)


def pair_elements(store, owner, val_energy, cond_bands, cond_energy, gvec_index):
    bands, _, side, plane = cond_bands.shape
    count = gvec_index.shape[0]
    pairs = bands // 2
    chunks = plane // WIDTH
    first_high, first_low, left = tables(side)
    spot = gvec_index % side * side + gvec_index // side % side
    kx = (gvec_index // plane).astype(F32)[None, :]
    total_bands = bands * lax.axis_size("col") * lax.axis_size("val")
    constant = total_bands ** (-0.25) * side ** (-1.5)
    vmem = pl.BlockSpec(memory_space=pltpu.VMEM)
    smem = pl.BlockSpec(memory_space=pltpu.SMEM)
    grid = pl.pallas_call(
        functools.partial(spread_kernel, side),
        out_shape=jax.ShapeDtypeStruct((2 * pairs, plane, LANES), F32),
        in_specs=[smem, vmem, pl.BlockSpec(memory_space=pl.ANY)] + [vmem] * 3,
        out_specs=vmem,
        scratch_shapes=[
            pltpu.VMEM((plane, 2 * pairs * LANES), F32),
            pltpu.VMEM(cond_bands.shape, F32),
            pltpu.VMEM((3, 2, chunks, side, WIDTH), F32),
            pltpu.VMEM((chunks, side, WIDTH), F32),
            pltpu.VMEM((2, chunks, side, WIDTH), F32),
            pltpu.SemaphoreType.DMA((4, chunks)),
            pltpu.SemaphoreType.DMA((4, chunks)),
            pltpu.SemaphoreType.DMA,
        ],
        compiler_params=pltpu.CompilerParams(
            vmem_limit_bytes=60 * 1024 * 1024, collective_id=0, has_side_effects=True
        ),
    )(owner, store, cond_bands, first_high, first_low, left)
    return pl.pallas_call(
        functools.partial(pick_kernel, side, bands, constant),
        out_shape=jax.ShapeDtypeStruct((2 * bands, count), BF16),
        in_specs=[smem] * 3 + [vmem] * 4,
        out_specs=vmem,
        scratch_shapes=[
            pltpu.VMEM((plane * 8, LANES), F32),
            pltpu.VMEM((512 * 8, LANES), F32),
        ],
        compiler_params=pltpu.CompilerParams(vmem_limit_bytes=60 * 1024 * 1024),
    )(spot, val_energy, cond_energy, grid, left, picker(side, pairs), kx)


def local(valence_store, band_owner, valence_energy, cond_bands, cond_energy, gvec_index):
    bands, _, side, plane = cond_bands.shape
    n_val, n_col = lax.axis_size("val"), lax.axis_size("col")
    picked = pair_elements(
        valence_store[0, 0], band_owner, valence_energy, cond_bands, cond_energy, gvec_index
    )
    count = picked.shape[1]
    cols = count // n_col
    columns = picked.reshape(2 * bands, n_col, cols).transpose(1, 0, 2)
    columns = jnp.broadcast_to(columns[None], (n_val, n_col, 2 * bands, cols))
    rows = picked[:, : ROW_DEV * n_val].reshape(2 * bands, n_val, ROW_DEV).transpose(1, 0, 2)
    rows = jnp.broadcast_to(rows[:, None], (n_val, n_col, 2 * bands, ROW_DEV))
    message = jnp.concatenate([columns, rows], 3).reshape(n_val * n_col, 2 * bands, cols + ROW_DEV)
    message = lax.all_to_all(message, ("val", "col"), split_axis=0, concat_axis=0, tiled=True)
    message = message.reshape(n_val * n_col, 2, bands, cols + ROW_DEV).transpose(1, 0, 2, 3)
    message = message.reshape(2, n_val * n_col * bands, cols + ROW_DEV)
    columns, rows = message[:, :, :cols], message[:, :, cols:]
    row_re, row_im = rows[0], rows[1]
    both = jnp.concatenate([rows[0], rows[1]], 0)
    turned = jnp.concatenate([rows[1], -rows[0]], 0)
    flat = columns.reshape(-1, cols)
    return -jnp.stack([dot(both, flat, ((0,), (0,))), dot(turned, flat, ((0,), (0,)))])


def solution(mesh):
    return jax.shard_map(
        local,
        mesh=mesh,
        in_specs=(
            P("val", "col", None, None, None),
            P(),
            P("val"),
            P("col", None, None, None),
            P("col"),
            P(),
        ),
        out_specs=P(None, "val", "col"),
        check_vma=False,
    )
```

```python
import functools
import math

import jax
import jax.numpy as jnp
import ml_dtypes
import numpy as np
from jax import lax
from jax.experimental import pallas as pl
from jax.experimental.pallas import tpu as pltpu
from jax.sharding import PartitionSpec as P

ROW_DEV = 64
LANES = 128
WIDTH = 256
MESH = pl.DeviceIdType.MESH
BF16 = jnp.bfloat16
F32 = jnp.float32


def split_table(table):
    high = table.astype(ml_dtypes.bfloat16)
    low = (table - high.astype(np.float64)).astype(ml_dtypes.bfloat16)
    return high, low


def tables(side):
    counter = np.arange(side)
    angles = 2.0 * math.pi * ((counter[:, None] * counter[None, :]) % side) / side
    cosine, sine = np.cos(angles), np.sin(angles)
    first = np.zeros((2, 2, side, 2, LANES))
    for band in range(2):
        span = slice(band * side, (band + 1) * side)
        first[band, 0, :, 0, span] = cosine
        first[band, 1, :, 0, span] = sine
        first[band, 1, :, 1, span] = cosine
        first[band, 0, :, 1, span] = -sine
    first_high, first_low = split_table(first.reshape(4 * side, 2 * LANES))
    both_high, both_low = split_table(np.concatenate([cosine, sine], 0))
    left = np.concatenate([both_high, both_high, both_low], 1)
    return first_high, first_low, left


def picker(side, pairs):
    table = np.zeros((2, pairs, LANES, LANES))
    for part in range(2):
        for pair in range(pairs):
            for band in range(2):
                table[part, pair, band * side : (band + 1) * side, (part * pairs + pair) * 2 + band] = 1.0
    return table.reshape(2 * pairs * LANES, LANES).astype(ml_dtypes.bfloat16)


def split(value):
    high = value.astype(BF16)
    return high, (value - high.astype(F32)).astype(BF16)


def dot(left, right, dims=((1,), (0,))):
    return lax.dot_general(left, right, (dims, ((), ())), preferred_element_type=F32)


def turn(side, left_ref, block):
    half = block.shape[1] // 2
    high, low = split(block)
    both = dot(left_ref[...], jnp.concatenate([high, low, high], 0))
    real = both[:side, :half] + both[side:, half:]
    imag = both[:side, half:] - both[side:, :half]
    return real, imag


def spread_kernel(
    side, owner_ref, store_ref, cond_hbm, first_high_ref, first_low_ref, left_ref, grid_b,
    grid_a, cond_ref, streams, mine, valence_ref, send_sems, recv_sems, cond_sem,
):
    bands = cond_ref.shape[0]
    pairs = bands // 2
    plane = side * side
    half = pairs * LANES
    chunks = plane // WIDTH

    cond_copy = pltpu.make_async_copy(cond_hbm, cond_ref, cond_sem)
    cond_copy.start()

    n_col = lax.axis_size("col")
    me = lax.axis_index("col")
    chips = n_col // 2
    chip, core = me // 2, me % 2
    sibling = me + 1 - 2 * core
    right = jnp.minimum(me + 2, n_col - 2 + core)
    left = jnp.maximum(me - 2, core)
    has_left, has_right = chip > 0, chip < chips - 1

    barrier = pltpu.get_barrier_semaphore()
    pl.semaphore_signal(barrier, inc=1, device_id={"col": sibling}, device_id_type=MESH)

    @pl.when(has_left)
    def _():
        pl.semaphore_signal(barrier, inc=1, device_id={"col": left}, device_id_type=MESH)

    @pl.when(has_right)
    def _():
        pl.semaphore_signal(barrier, inc=1, device_id={"col": right}, device_id_type=MESH)

    pl.semaphore_wait(barrier, 3 - (chip == 0).astype(jnp.int32) - (chip == chips - 1).astype(jnp.int32))

    def copy(kind, k):
        peer = (sibling, right, left)[kind]
        return pltpu.make_async_remote_copy(
            src_ref=streams.at[kind, 0, k],
            dst_ref=streams.at[kind, 1, k],
            send_sem=send_sems.at[kind, k],
            recv_sem=recv_sems.at[kind, k],
            device_id={"col": peer},
            device_id_type=MESH,
        )

    def final_copy(part, k):
        return pltpu.make_async_remote_copy(
            src_ref=valence_ref.at[part, k],
            dst_ref=valence_ref.at[part, k],
            send_sem=send_sems.at[3, k],
            recv_sem=recv_sems.at[3, k],
            device_id={"col": sibling},
            device_id_type=MESH,
        )

    def lanes_of(k):
        return pl.ds(pl.multiple_of(k * WIDTH, WIDTH), WIDTH)

    gap = jnp.full((1, WIDTH), owner_ref[lax.axis_index("val")] - me).astype(F32)
    owned = jnp.maximum(1.0 - gap * gap, 0.0)

    @pl.loop(0, chunks)
    def _(k):
        streams[0, 0, k] = store_ref[1 - core, :, lanes_of(k)] * owned
        copy(0, k).start()

    @pl.when(jnp.logical_not(has_left))
    def _():
        streams[1, 1] = jnp.zeros((chunks, side, WIDTH), F32)

    @pl.when(jnp.logical_not(has_right))
    def _():
        streams[2, 1] = jnp.zeros((chunks, side, WIDTH), F32)

    def pass_on(kind, k, has_source, has_target):
        @pl.when(has_source)
        def _():
            copy(kind, k).wait_recv()

        @pl.when(has_target)
        def _():
            streams[kind, 0, k] = mine[k] + streams[kind, 1, k]
            copy(kind, k).start()

    def first_axis(k):
        v_re, v_im = valence_ref[0, k], valence_ref[1, k]
        lanes = lanes_of(k)
        for pair in range(pairs):
            parts = []
            for band in (2 * pair, 2 * pair + 1):
                c_re, c_im = cond_ref[band, 0, :, lanes], cond_ref[band, 1, :, lanes]
                parts += [v_re * c_re + v_im * c_im, v_re * c_im - v_im * c_re]
            high, low = split(jnp.concatenate(parts, 0).T)
            result = (
                dot(high, first_high_ref[...])
                + dot(low, first_high_ref[...])
                + dot(high, first_low_ref[...])
            )
            grid_a[lanes, pair * LANES : (pair + 1) * LANES] = result[:, :LANES]
            grid_a[lanes, half + pair * LANES : half + (pair + 1) * LANES] = result[:, LANES:]

    def last_axis(y):
        rows = pl.ds(pl.multiple_of(y * side, 8), side)
        real, imag = turn(side, left_ref, grid_a[rows, :])
        for pair in range(pairs):
            span = slice(pair * LANES, (pair + 1) * LANES)
            grid_b[pair, rows, :] = real[:, span]
            grid_b[pairs + pair, rows, :] = imag[:, span]

    right_lag = 2 * chip
    left_lag = 2 * (chips - 1 - chip)
    lag = jnp.maximum(right_lag, left_lag)
    cond_copy.wait()

    @pl.loop(0, chunks + lag + 1)
    def _(step):
        @pl.when(step < chunks)
        def _():
            copy(0, step).wait_recv()
            mine[step] = streams[0, 1, step] + store_ref[core, :, lanes_of(step)] * owned

        @pl.when((step >= right_lag) & (step - right_lag < chunks))
        def _():
            pass_on(1, step - right_lag, has_left, has_right)

        @pl.when((step >= left_lag) & (step - left_lag < chunks))
        def _():
            pass_on(2, step - left_lag, has_right, has_left)

        @pl.when((step >= lag) & (step - lag < chunks))
        def _():
            k = step - lag
            valence_ref[core, k] = mine[k] + streams[1, 1, k] + streams[2, 1, k]
            final_copy(core, k).start()

        @pl.when(step > lag)
        def _():
            k = step - lag - 1
            final_copy(1 - core, k).wait_recv()
            first_axis(k)

            @pl.loop(k * WIDTH // side, (k + 1) * WIDTH // side)
            def _(y):
                last_axis(y)

    @pl.loop(0, chunks)
    def _(k):
        copy(0, k).wait_send()
        final_copy(core, k).wait_send()

        @pl.when(has_right)
        def _():
            copy(1, k).wait_send()

        @pl.when(has_left)
        def _():
            copy(2, k).wait_send()


def pick_kernel(
    side, bands, scale_constant, rows_ref, val_energy_ref, energy_ref, grid_b, left_ref,
    picker_ref, kx_ref, out_ref, spots, chosen,
):
    pairs = bands // 2

    @pl.loop(0, side)
    def _(kz):
        block = jnp.concatenate(
            [grid_b[part, pl.ds(kz, side, stride=side), :] for part in range(2 * pairs)], 1
        )
        real, imag = turn(side, left_ref, block)
        for pair in range(pairs):
            span = slice(pair * LANES, (pair + 1) * LANES)
            base = kz * side * 8
            spots[pl.ds(base + pair, side, stride=8), :] = real[:, span]
            spots[pl.ds(base + pairs + pair, side, stride=8), :] = imag[:, span]

    n_val, n_col = out_ref.shape[0], out_ref.shape[1]
    chunk = out_ref.shape[3] - ROW_DEV
    row = lax.broadcasted_iota(jnp.int32, (2 * bands, LANES), 0) % bands
    energy = jnp.zeros((2 * bands, LANES), F32)
    for band in range(bands):
        energy = jnp.where(row == band, energy_ref[band], energy)
    scale = jnp.sqrt(2.0 / (energy - val_energy_ref[0])) * scale_constant
    lane = lax.broadcasted_iota(jnp.int32, (1, LANES), 1)
    lane = jnp.where(lane < side, lane, jnp.where(lane < 2 * side, lane - side, -1)).astype(F32)

    @pl.loop(0, n_col)
    def _(step):
        base = step * chunk

        @pl.loop(0, chunk // 32)
        def _(inner):
            for item in range(32):
                spot = pl.multiple_of(rows_ref[base + inner * 32 + item] * 8, 8)
                to = pl.multiple_of((inner * 32 + item) * 8, 8)
                chosen[pl.ds(to, 8), :] = spots[pl.ds(spot, 8), :]

        where = pl.ds(pl.multiple_of(base, chunk), chunk)
        wanted = jnp.broadcast_to(kx_ref[:, where], (LANES, chunk)).T
        mask = wanted == lane
        total = jnp.zeros((chunk, LANES), F32)
        for part in range(2 * pairs):
            value = jnp.where(mask, chosen[pl.ds(part, chunk, stride=8), :], 0.0)
            high, low = split(value)
            table = picker_ref[part * LANES : (part + 1) * LANES, :]
            total += dot(high, table) + dot(low, table)
        values = (total.T[: 2 * bands, :] * scale[:, :1]).astype(BF16)
        for index in range(n_val):
            out_ref[index, step, :, :chunk] = values

            @pl.when(step == index * ROW_DEV // chunk)
            def _(index=index):
                offset = index * ROW_DEV % chunk
                for target in range(n_col):
                    out_ref[index, target, :, chunk:] = values[:, offset : offset + ROW_DEV]


def pair_elements(store, owner, val_energy, cond_bands, cond_energy, gvec_index):
    bands, _, side, plane = cond_bands.shape
    count = gvec_index.shape[0]
    pairs = bands // 2
    chunks = plane // WIDTH
    first_high, first_low, left = tables(side)
    spot = gvec_index % side * side + gvec_index // side % side
    kx = (gvec_index // plane).astype(F32)[None, :]
    n_val, n_col = lax.axis_size("val"), lax.axis_size("col")
    cols = count // n_col
    total_bands = bands * n_col * n_val
    constant = total_bands ** (-0.25) * side ** (-1.5)
    vmem = pl.BlockSpec(memory_space=pltpu.VMEM)
    smem = pl.BlockSpec(memory_space=pltpu.SMEM)
    grid = pl.pallas_call(
        functools.partial(spread_kernel, side),
        out_shape=jax.ShapeDtypeStruct((2 * pairs, plane, LANES), F32),
        in_specs=[smem, vmem, pl.BlockSpec(memory_space=pl.ANY)] + [vmem] * 3,
        out_specs=vmem,
        scratch_shapes=[
            pltpu.VMEM((plane, 2 * pairs * LANES), F32),
            pltpu.VMEM(cond_bands.shape, F32),
            pltpu.VMEM((3, 2, chunks, side, WIDTH), F32),
            pltpu.VMEM((chunks, side, WIDTH), F32),
            pltpu.VMEM((2, chunks, side, WIDTH), F32),
            pltpu.SemaphoreType.DMA((4, chunks)),
            pltpu.SemaphoreType.DMA((4, chunks)),
            pltpu.SemaphoreType.DMA,
        ],
        compiler_params=pltpu.CompilerParams(
            vmem_limit_bytes=60 * 1024 * 1024, collective_id=0, has_side_effects=True
        ),
    )(owner, store, cond_bands, first_high, first_low, left)
    return pl.pallas_call(
        functools.partial(pick_kernel, side, bands, constant),
        out_shape=jax.ShapeDtypeStruct((n_val, n_col, 2 * bands, cols + ROW_DEV), BF16),
        in_specs=[smem] * 3 + [vmem] * 4,
        out_specs=vmem,
        scratch_shapes=[
            pltpu.VMEM((plane * 8, LANES), F32),
            pltpu.VMEM((cols * 8, LANES), F32),
        ],
        compiler_params=pltpu.CompilerParams(vmem_limit_bytes=60 * 1024 * 1024),
    )(spot, val_energy, cond_energy, grid, left, picker(side, pairs), kx)


def local(valence_store, band_owner, valence_energy, cond_bands, cond_energy, gvec_index):
    bands, _, side, plane = cond_bands.shape
    n_val, n_col = lax.axis_size("val"), lax.axis_size("col")
    message = pair_elements(
        valence_store[0, 0], band_owner, valence_energy, cond_bands, cond_energy, gvec_index
    )
    cols = message.shape[3] - ROW_DEV
    message = message.reshape(n_val * n_col, 2 * bands, cols + ROW_DEV)
    message = lax.all_to_all(message, ("val", "col"), split_axis=0, concat_axis=0, tiled=True)
    message = message.reshape(n_val * n_col, 2, bands, cols + ROW_DEV).transpose(1, 0, 2, 3)
    message = message.reshape(2, n_val * n_col * bands, cols + ROW_DEV)
    columns, rows = message[:, :, :cols], message[:, :, cols:]
    row_re, row_im = rows[0], rows[1]
    both = jnp.concatenate([rows[0], rows[1]], 0)
    turned = jnp.concatenate([rows[1], -rows[0]], 0)
    flat = columns.reshape(-1, cols)
    return -jnp.stack([dot(both, flat, ((0,), (0,))), dot(turned, flat, ((0,), (0,)))])


def solution(mesh):
    return jax.shard_map(
        local,
        mesh=mesh,
        in_specs=(
            P("val", "col", None, None, None),
            P(),
            P("val"),
            P("col", None, None, None),
            P("col"),
            P(),
        ),
        out_specs=P(None, "val", "col"),
        check_vma=False,
    )
```
